32 devices in a mesh: pipe: 8 (over z, y), expert: 4 (over x, core).
Axes of the slice: x: 2, y: 2, z: 4, core: 2. Of those that a mesh axis runs over, the one named last changes fastest.
Arguments:
- fwd_in: bfloat16 [4096, 3584], P(('pipe', 'expert')), may hold values from -6 to 6
- fwd_routes: int32 [4096, 2], P(('pipe', 'expert')), may hold values from 0 to 3, all different within a row; in each aligned block of 128 rows (0 to 127, 128 to 255, ...) at most 96 rows name the same one
- saved_in: bfloat16 [4096, 3584], P(('pipe', 'expert')), may hold values from -6 to 6
- saved_routes: int32 [4096, 2], P(('pipe', 'expert')), may hold values from 0 to 3, all different within a row; in each aligned block of 128 rows (0 to 127, 128 to 255, ...) at most 96 rows name the same one
- grad_in: bfloat16 [4096, 3584], P(('pipe', 'expert')), may hold values from -6 to 6
- norm_gain: float32 [8, 3584], P('pipe'), may hold values from 0.25 to 1.75
- router: bfloat16 [8, 3584, 4], P('pipe'), may hold values from -0.09375 to 0.09375
- w_gate: bfloat16 [8, 4, 3584, 1024], P('pipe', 'expert'), may hold values from -0.09375 to 0.09375
- w_up: bfloat16 [8, 4, 3584, 1024], P('pipe', 'expert'), may hold values from -0.09375 to 0.09375
- w_down: bfloat16 [8, 4, 1024, 3584], P('pipe', 'expert'), may hold values from -0.1875 to 0.1875
Outputs:
- fwd_out: bfloat16 [4096, 3584], P(('pipe', 'expert'))
- grad_out: bfloat16 [4096, 3584], P(('pipe', 'expert'))
The draws below stay inside these ranges and needn't reach their ends.
Inputs may be any that keep to these rules, and one draw needn't show every extreme that they name: `fwd_routes`: each row names 2 different experts; among the rows of one device no expert is named by more than 96 rows, a bound that some block reaches. `saved_routes`: each row names 2 different experts; among the rows of one device no expert is named by more than 96 rows, a bound that some block reaches.
All inputs are finite; a program needn't handle non-finite values.
Results may differ from the reference program's by a relative error of at most 0.0057.
Values may be sent and summed in bfloat16 or wider, within the bound.
No kernel may reach another device: no remote copies, remote signals or barrier semaphores. Data moves between devices by JAX's collectives and lax.ppermute only.
A program may use at most 128 MiB of HBM per device.

```python
import math
import jax
import jax.numpy as jnp
import numpy as np
from jax import lax

D = 3584
F = 1024
TOP = 2
TOK_DEV = 128
EXPERTS = 4
CAP = 96
TOKENS = 4096
N_PIPE = 8
N_EXPERT = 4


def steps_of(key, shape, shards, smallest, largest):
    gain, own = 1.0, jax.random.fold_in(key, 6)
    for dim, blocks in shards:
        draws = jnp.exp(jax.random.uniform(jax.random.fold_in(own, dim), (blocks,), jnp.float32, smallest / len(shards), largest / len(shards)))
        gain = gain * jnp.repeat(draws, shape[dim] // blocks).reshape([-1 if axis == dim else 1 for axis in range(len(shape))])
    return gain


def routed_block(stream_key, own, number, rows, number_of, top, bound, skew):
    sequence = jax.random.permutation(stream_key, number_of)
    crowded, common = portions_of(number_of, rows * top, bound, skew, True), portions_of(number_of, rows * top, bound, skew, False)
    places = jnp.arange(number_of)

    def named(lengths, turn):
        used = int((lengths > 0).sum())
        fixed = max(1, used // 4)
        passed = fixed + (places - fixed + turn * (used - fixed)) % max(1, number_of - fixed)
        return jnp.zeros((number_of,), jnp.int32).at[sequence[jnp.where(places < fixed, places, passed)]].set(jnp.asarray(lengths, jnp.int32))

    lengths = jnp.where(number % 4 == 0, named(crowded, number // 4), named(common, number - number // 4 - 1))
    mixed = jax.random.permutation(jax.random.fold_in(own, 3), number_of)
    donor, sink = mixed[0:number_of // 2 * 2:2], mixed[1:number_of // 2 * 2:2]
    slack = jnp.minimum(lengths[donor] - 1, bound - lengths[sink]) // 2
    slack = jnp.where((donor == sequence[0]) | (sink == sequence[0]) | (lengths[sink] == 0), 0, jnp.maximum(slack, 0))
    passed = jax.random.randint(jax.random.fold_in(own, 4), (number_of // 2,), 0, 1 << 20) % (slack + 1)
    lengths = lengths.at[donor].add(-passed).at[sink].add(passed)
    members = jnp.searchsorted(jnp.cumsum(lengths), jnp.arange(rows * top), side="right").astype(jnp.int32)
    grid = members.reshape(top, rows).T
    grid = grid[jax.random.permutation(jax.random.fold_in(own, 1), rows)]
    turn = jax.random.randint(jax.random.fold_in(own, 2), (rows, 1), 0, top)
    return jnp.take_along_axis(grid, (jnp.arange(top)[None, :] + turn) % top, axis=1)


def portions_of(count, total, most, skew, full):
    loads = [(1 << 20) // math.isqrt(rank ** skew) + 1 for rank in range(1, count + 1)]
    largest = most if full else min(most, max(-(-total // count), total * loads[0] // sum(loads)))
    least = 1 if total - largest >= count - 1 else 0
    counts, surplus = [largest] + [least] * (count - 1), total - largest - least * (count - 1)
    while surplus > 0:
        movable = [i for i in range(1, count) if counts[i] < largest] or [i for i in range(1, count) if counts[i] < most]
        whole, remaining = sum([loads[i] for i in movable]), surplus
        for i in movable:
            more = min(most - counts[i], max(1, remaining * loads[i] // whole), surplus)
            counts[i] = counts[i] + more
            surplus = surplus - more
    return np.array(counts)


def noise(rng, dims, spread, most, shards=(), kind=jnp.bfloat16):
    factor_of = steps_of(rng, dims, shards, -0.22, 0.18) if shards else 1.0
    values = jax.random.normal(rng, dims, jnp.float32) * spread * factor_of
    return jnp.minimum(jnp.maximum(values, -most), most).astype(kind)


def setup_inputs(seed: int = 0) -> dict:
    splits = jax.random.split(jax.random.key(seed), 11)
    fwd_in = noise(splits[0], (TOKENS, D), 1.0, 6.0, ((0, 32),))
    fwd_routes_keys = jax.random.split(jax.random.fold_in(splits[1], 1), TOKENS // TOK_DEV)
    fwd_routes_turns = jax.random.permutation(jax.random.fold_in(splits[1], 3), TOKENS // TOK_DEV)
    fwd_routes = jax.vmap(lambda own, number: routed_block(jax.random.fold_in(splits[1], 2), own, number, TOK_DEV, EXPERTS, TOP, CAP, 1))(fwd_routes_keys, fwd_routes_turns).reshape((TOKENS, TOP))
    saved_in = noise(splits[2], (TOKENS, D), 1.0, 6.0, ((0, 32),))
    saved_routes_keys = jax.random.split(jax.random.fold_in(splits[3], 1), TOKENS // TOK_DEV)
    saved_routes_turns = jax.random.permutation(jax.random.fold_in(splits[3], 3), TOKENS // TOK_DEV)
    saved_routes = jax.vmap(lambda own, number: routed_block(jax.random.fold_in(splits[3], 2), own, number, TOK_DEV, EXPERTS, TOP, CAP, 1))(saved_routes_keys, saved_routes_turns).reshape((TOKENS, TOP))
    grad_in = noise(splits[4], (TOKENS, D), 1.0, 6.0, ((0, 32),))
    norm_gain = jnp.clip(1.0 + 0.15 * jax.random.normal(splits[5], (N_PIPE, D), jnp.float32), 0.25, 1.75)
    router = noise(splits[6], (N_PIPE, D, EXPERTS), D ** -0.5, 0.09375, ((0, 8),))
    w_gate = noise(splits[7], (N_PIPE, EXPERTS, D, F), D ** -0.5, 0.09375, ((0, 8), (1, 4)))
    w_up = noise(splits[8], (N_PIPE, EXPERTS, D, F), D ** -0.5, 0.09375, ((0, 8), (1, 4)))
    w_down = noise(splits[9], (N_PIPE, EXPERTS, F, D), F ** -0.5, 0.1875, ((0, 8), (1, 4)))
    return {"fwd_in": fwd_in, "fwd_routes": fwd_routes, "saved_in": saved_in, "saved_routes": saved_routes, "grad_in": grad_in, "norm_gain": norm_gain, "router": router, "w_gate": w_gate, "w_up": w_up, "w_down": w_down}


EPSILON = 1e-06

def normalize(in_rows, gain_row):
    widened = in_rows.astype(jnp.float32)
    inv_rms = lax.rsqrt(lax.optimization_barrier(jnp.mean(widened * widened, axis=-1, keepdims=True)) + EPSILON)
    normed = (widened * inv_rms * gain_row).astype(jnp.bfloat16)
    return (widened, inv_rms, normed)

def route_weights(normed, router_cols, route_ids):
    logits = jnp.dot(normed, router_cols, preferred_element_type=jnp.float32)
    scores = jax.nn.sigmoid(logits)
    expert_ids = jnp.arange(router_cols.shape[1], dtype=jnp.int32)
    picked = (route_ids[:, :, None] == expert_ids[None, None, :]).astype(jnp.float32)
    chosen = lax.optimization_barrier(jnp.sum(picked * scores[:, None, :], axis=-1))
    summed = lax.optimization_barrier(jnp.sum(chosen, axis=-1, keepdims=True))
    return (picked, chosen, summed, chosen / summed)

def expert_forward(normed, gate_w, up_w, down_w):
    gate_pre = jnp.dot(normed, gate_w, preferred_element_type=jnp.float32)
    up_pre = jnp.dot(normed, up_w, preferred_element_type=jnp.float32)
    hidden = (jax.nn.silu(gate_pre) * up_pre).astype(jnp.bfloat16)
    output = jnp.dot(hidden, down_w, preferred_element_type=jnp.float32).astype(jnp.bfloat16)
    return (gate_pre, up_pre, output)

def expert_backward(normed, grad_rows, gate_w, up_w, down_w):
    gate_pre, up_pre, output = expert_forward(normed, gate_w, up_w, down_w)
    dhidden = jnp.dot(grad_rows, down_w.T, preferred_element_type=jnp.float32)
    sigmoid_gate = jax.nn.sigmoid(gate_pre)
    dgate = (dhidden * up_pre * sigmoid_gate * (1.0 + gate_pre * (1.0 - sigmoid_gate))).astype(jnp.bfloat16)
    dupper = (dhidden * jax.nn.silu(gate_pre)).astype(jnp.bfloat16)
    dnormed = (jnp.dot(dgate, gate_w.T, preferred_element_type=jnp.float32) + jnp.dot(dupper, up_w.T, preferred_element_type=jnp.float32)).astype(jnp.bfloat16)
    dprob = lax.optimization_barrier(jnp.sum(grad_rows.astype(jnp.float32) * output.astype(jnp.float32), axis=-1)).astype(jnp.bfloat16)
    return (dnormed, dprob)

def input_gradient(grad_rows, widened, inv_rms, gain_row, router_cols, picked, chosen, summed, probs, dnorm_all, dprob_all):
    mixed_dot = lax.optimization_barrier(jnp.sum(dprob_all * probs, axis=-1, keepdims=True))
    dchosen = (dprob_all - mixed_dot) / summed
    dlogit_sel = dchosen * chosen * (1.0 - chosen)
    dlogits = lax.optimization_barrier(jnp.sum(picked * dlogit_sel[:, :, None], axis=1))
    dnorm_all = dnorm_all + jnp.dot(dlogits, router_cols.astype(jnp.float32).T, precision=lax.Precision.HIGHEST)
    scaled_grad = dnorm_all * gain_row
    dinput = inv_rms * scaled_grad - widened * inv_rms ** 3 * lax.optimization_barrier(jnp.mean(scaled_grad * widened, axis=-1, keepdims=True))
    return (grad_rows.astype(jnp.float32) + dinput).astype(jnp.bfloat16)

def expert_rows(route_ids, expert, limit):
    is_hit = jnp.any(route_ids == expert, axis=-1)
    picked_rows = jnp.nonzero(is_hit, size=limit, fill_value=0)[0].astype(jnp.int32)
    hit_count = jnp.sum(is_hit.astype(jnp.int32))
    is_valid = (jnp.arange(limit, dtype=jnp.int32) < hit_count).astype(jnp.float32)
    return (picked_rows, is_valid)

def group_forward(in_rows, route_ids, gain_row, router_cols, gate_mats, up_mats, down_mats):
    widened, inv_rms, normed = normalize(in_rows, gain_row)
    picked, chosen, summed, probs = route_weights(normed, router_cols, route_ids)
    result = widened
    limit = N_EXPERT * CAP
    for expert in range(EXPERTS):
        picked_rows, is_valid = expert_rows(route_ids, expert, limit)
        weight = lax.optimization_barrier(jnp.sum(picked[:, :, expert] * probs, axis=-1))[picked_rows] * is_valid
        _, _, output = expert_forward(normed[picked_rows], gate_mats[expert], up_mats[expert], down_mats[expert])
        result = result.at[picked_rows].add(weight[:, None] * output.astype(jnp.float32))
    return result.astype(jnp.bfloat16)

def group_backward(in_rows, route_ids, grad_rows, gain_row, router_cols, gate_mats, up_mats, down_mats):
    widened, inv_rms, normed = normalize(in_rows, gain_row)
    picked, chosen, summed, probs = route_weights(normed, router_cols, route_ids)
    row_count = in_rows.shape[0]
    dnorm_all = jnp.zeros(in_rows.shape, jnp.float32)
    dprob_all = jnp.zeros(route_ids.shape, jnp.float32)
    limit = N_EXPERT * CAP
    for expert in range(EXPERTS):
        picked_rows, is_valid = expert_rows(route_ids, expert, limit)
        weight = lax.optimization_barrier(jnp.sum(picked[:, :, expert] * probs, axis=-1))[picked_rows] * is_valid
        dnormed, dprob = expert_backward(normed[picked_rows], grad_rows[picked_rows], gate_mats[expert], up_mats[expert], down_mats[expert])
        dnorm_all = dnorm_all.at[picked_rows].add(weight[:, None] * dnormed.astype(jnp.float32))
        dprob_rows = jnp.zeros((row_count,), jnp.float32).at[picked_rows].add(is_valid * dprob.astype(jnp.float32))
        dprob_all = dprob_all + picked[:, :, expert] * dprob_rows[:, None]
    return input_gradient(grad_rows, widened, inv_rms, gain_row, router_cols, picked, chosen, summed, probs, dnorm_all, dprob_all)

def reference(fwd_in, fwd_routes, saved_in, saved_routes, grad_in, norm_gain, router, w_gate, w_up, w_down):
    section_rows = TOK_DEV * N_EXPERT

    def one_section(section_args):
        f_rows, f_ids, s_rows, s_ids, g_rows, gain_row, router_cols, gate_mats, up_mats, down_mats = section_args
        forward = group_forward(f_rows, f_ids, gain_row, router_cols, gate_mats, up_mats, down_mats)
        backward = group_backward(s_rows, s_ids, g_rows, gain_row, router_cols, gate_mats, up_mats, down_mats)
        return (forward, backward)
    stacked = (fwd_in.reshape(N_PIPE, section_rows, D), fwd_routes.reshape(N_PIPE, section_rows, TOP), saved_in.reshape(N_PIPE, section_rows, D), saved_routes.reshape(N_PIPE, section_rows, TOP), grad_in.reshape(N_PIPE, section_rows, D), norm_gain, router, w_gate, w_up, w_down)
    forward_all, backward_all = lax.map(one_section, stacked)
    zero_block = jnp.zeros((1, section_rows, D), jnp.bfloat16)
    fwd_out = jnp.concatenate([zero_block, forward_all[:-1]], axis=0).reshape(TOKENS, D)
    grad_out = jnp.concatenate([backward_all[1:], zero_block], axis=0).reshape(TOKENS, D)
    return (fwd_out, grad_out)
```

```python
import functools

import jax
import jax.numpy as jnp
from jax import lax
from jax.experimental import pallas as pl
from jax.experimental.pallas import tpu as pltpu
from jax.sharding import PartitionSpec as P

EPSILON = 1e-06
LANES = 128
BLOCK = 256
OUT = 896
CHUNK = 64
AHEAD = 4
NT = (((1,), (1,)), ((), ()))
F32 = jnp.float32
BF16 = jnp.bfloat16


def matmul(a, b):
    return jnp.dot(a, b, preferred_element_type=F32)


def matmul_nt(a, b):
    return lax.dot_general(a, b, NT, preferred_element_type=F32)


def load(src, dst, sem):
    copy = pltpu.make_async_copy(src, dst, sem)
    copy.start()
    return copy


def load_pair(a, b, dst, sems, first):
    rows = a.shape[0]
    return [
        load(a, dst.at[pl.ds(0, rows)], sems.at[first]),
        load(b, dst.at[pl.ds(rows, rows)], sems.at[first + 1]),
    ]


def wait(copies):
    for copy in copies:
        copy.wait()


def normalize_rows(xs, gain_ref, normed, inv):
    for at in range(0, xs.shape[0], CHUNK):
        rows = slice(at, at + CHUNK)
        wide = xs[rows, :].astype(F32)
        r = lax.rsqrt(jnp.mean(wide * wide, axis=-1, keepdims=True) + EPSILON)
        inv[rows, :] = jnp.broadcast_to(r, (CHUNK, LANES))
        normed[rows, :] = (xs[rows, :].astype(F32) * r * gain_ref[...]).astype(BF16)


def routing(me, ids, router_ref, router_pad, normed, first):
    router_pad[...] = jnp.zeros_like(router_pad)
    router_pad[0 : router_ref.shape[0], :] = router_ref[...]
    scores = jax.nn.sigmoid(matmul_nt(normed[...], router_pad[...]))
    column = lax.broadcasted_iota(jnp.int32, scores.shape, 1)
    chosen = (column == ids[:, first : first + 1]) | (column == ids[:, first + 1 : first + 2])
    chosen = chosen.astype(F32)
    mine = chosen * (column == me).astype(F32)
    summed = jnp.sum(chosen * scores, axis=-1, keepdims=True)
    prob = jnp.sum(mine * scores, axis=-1, keepdims=True) / summed
    return scores, chosen, mine, summed, prob


def forward_kernel(
    me_ref, xa, xb, ra, rb, gain, router, wg, wu, wd, oa, ob,
    xs, normed, inv, router_pad, wgv, wuv, wdv, hid, sem_x, sem_w,
):
    rows, width = xa.shape
    hidden = wg.shape[1]
    blocks = [pl.ds(at, BLOCK) for at in range(0, hidden, BLOCK)]
    outs = [pl.ds(at, OUT) for at in range(0, width, OUT)]

    def weights(step):
        if step < len(blocks):
            at = (slice(None), blocks[step])
            return [
                load(wg.at[at], wgv.at[at], sem_w.at[2 * step]),
                load(wu.at[at], wuv.at[at], sem_w.at[2 * step + 1]),
            ]
        at = (slice(None), outs[step - len(blocks)])
        return [load(wd.at[at], wdv.at[at], sem_w.at[len(blocks) + step])]

    steps = len(blocks) + len(outs)
    loads_x = load_pair(xa, xb, xs, sem_x, 0)
    loads_w = [weights(step) for step in range(AHEAD)]
    wait(loads_x)
    normalize_rows(xs, gain, normed, inv)
    ids = jnp.concatenate([ra[...], rb[...]], axis=0)
    prob = routing(me_ref[0], ids, router, router_pad, normed, 2)[4]
    for step in range(steps):
        wait(loads_w[step])
        if step + AHEAD < steps:
            loads_w.append(weights(step + AHEAD))
        if step < len(blocks):
            at = blocks[step]
            gate = matmul(normed[...], wgv[:, at])
            up = matmul(normed[...], wuv[:, at])
            hid[:, at] = (jax.nn.silu(gate) * up).astype(BF16)
        else:
            at = outs[step - len(blocks)]
            out = matmul(hid[...], wdv[:, at]).astype(BF16).astype(F32)
            out = (prob * out).astype(BF16)
            oa[:, at] = out[:rows]
            ob[:, at] = out[rows:]


def backward_kernel(
    me_ref, xa, xb, za, zb, ra, rb, gain, router, wg, wu, wd, oa, ob,
    xs, normed, inv, router_pad, wgv, wuv, wdv, dgs, zs, dus, vs, sem_x, sem_w,
):
    rows, width = xa.shape
    hidden = wg.shape[1]
    blocks = [pl.ds(at, BLOCK) for at in range(0, hidden, BLOCK)]
    outs = [pl.ds(at, OUT) for at in range(0, width, OUT)]

    def weights(step):
        at = (slice(None), blocks[step])
        down = (blocks[step], slice(None))
        return [
            load(wg.at[at], wgv.at[at], sem_w.at[3 * step]),
            load(wu.at[at], wuv.at[at], sem_w.at[3 * step + 1]),
            load(wd.at[down], wdv.at[down], sem_w.at[3 * step + 2]),
        ]

    loads_x = load_pair(xa, xb, xs, sem_x, 0)
    loads_z = load_pair(za, zb, zs, sem_x, 2)
    loads_w = [weights(step) for step in range(AHEAD)]
    wait(loads_x)
    normalize_rows(xs, gain, normed, inv)
    ids = jnp.concatenate([ra[...], rb[...]], axis=0)
    scores, chosen, mine, summed, prob = routing(
        me_ref[0], ids, router, router_pad, normed, 0
    )
    routed = jnp.sum(mine, axis=-1, keepdims=True)
    slope = routed * chosen * (mine - prob) / summed * scores * (1.0 - scores)
    wait(loads_z)
    product = jnp.zeros((2 * rows, 1), F32)
    for step, at in enumerate(blocks):
        wait(loads_w[step])
        if step + AHEAD < len(blocks):
            loads_w.append(weights(step + AHEAD))
        gate = matmul(normed[...], wgv[:, at])
        up = matmul(normed[...], wuv[:, at])
        dhidden = matmul_nt(zs[...], wdv[at, :])
        sig = jax.nn.sigmoid(gate)
        silu = gate * sig
        kept = (silu * up).astype(BF16).astype(F32)
        product += jnp.sum(kept * dhidden, axis=-1, keepdims=True)
        dgs[:, at] = (dhidden * up * sig * (1.0 + gate * (1.0 - sig))).astype(BF16)
        dus[:, at] = (dhidden * silu).astype(BF16)
    dlogits = slope * product.astype(BF16).astype(F32)
    high = dlogits.astype(BF16)
    low = (dlogits - high.astype(F32)).astype(BF16)
    mean = jnp.zeros((2 * rows, 1), F32)
    for at in outs:
        n = matmul_nt(dgs[...], wgv[at, :]) + matmul_nt(dus[...], wuv[at, :])
        m = prob * n.astype(BF16).astype(F32)
        m += matmul(high, router_pad[:, at]) + matmul(low, router_pad[:, at])
        v = m * gain[:, at]
        vs[:, at] = v
        mean += jnp.sum(v * xs[:, at].astype(F32), axis=-1, keepdims=True)
    r = inv[:, 0:1]
    shrink = r * r * r * (mean / width)
    for part, o_ref in enumerate((oa, ob)):
        for at in range(0, rows, CHUNK):
            src = slice(part * rows + at, part * rows + at + CHUNK)
            wide = xs[src, :].astype(F32)
            o_ref[at : at + CHUNK, :] = (r[src] * vs[src, :] - wide * shrink[src]).astype(BF16)


def expert_call(kernel, me, pairs, routes, gain, router, wg, wu, wd, backward):
    rows, width = pairs[0].shape
    hidden = wg.shape[1]
    both = 2 * rows
    steps = hidden // BLOCK
    vmem = pl.BlockSpec(memory_space=pltpu.VMEM)
    any_ = pl.BlockSpec(memory_space=pl.ANY)
    in_specs = [pl.BlockSpec(memory_space=pltpu.SMEM)] + [any_] * len(pairs)
    in_specs += [vmem] * (len(routes) + 2) + [any_] * 3
    out = jax.ShapeDtypeStruct((rows, width), BF16)
    scratch = [
        pltpu.VMEM((both, width), BF16),
        pltpu.VMEM((both, width), BF16),
        pltpu.VMEM((both, LANES), F32),
        pltpu.VMEM((LANES, width), BF16),
        pltpu.VMEM(wg.shape, BF16),
        pltpu.VMEM(wu.shape, BF16),
        pltpu.VMEM(wd.shape, BF16),
        pltpu.VMEM((both, hidden), BF16),
    ]
    copies = 2 * steps + width // OUT
    if backward:
        scratch += [
            pltpu.VMEM((both, width), BF16),
            pltpu.VMEM((both, hidden), BF16),
            pltpu.VMEM((both, width), F32),
        ]
        copies = 3 * steps
    scratch += [pltpu.SemaphoreType.DMA((len(pairs),)), pltpu.SemaphoreType.DMA((copies,))]
    return pl.pallas_call(
        kernel,
        out_shape=(out, out),
        in_specs=in_specs,
        out_specs=(vmem, vmem),
        scratch_shapes=scratch,
        compiler_params=pltpu.CompilerParams(vmem_limit_bytes=48 * 1024 * 1024),
        cost_estimate=pl.CostEstimate(flops=1, bytes_accessed=1, transcendentals=0),
    )(me, *pairs, *routes, gain, router, wg, wu, wd)


def swap(x, by):
    peers = lax.axis_size("expert")
    return lax.ppermute(x, "expert", [(i, i ^ by) for i in range(peers)])


def shifted(x, by, across):
    groups, peers = lax.axis_size("pipe"), lax.axis_size("expert")
    pairs = [
        (c * peers + i, (c + by) * peers + (i ^ across))
        for c in range(groups)
        if 0 <= c + by < groups
        for i in range(peers)
    ]
    return lax.ppermute(x, ("pipe", "expert"), pairs)


def added(*parts):
    total = parts[0].astype(F32)
    for part in parts[1:]:
        total = total + part.astype(F32)
    return total.astype(BF16)


def local(
    fwd_in, fwd_routes, saved_in, saved_routes, grad_in, norm_gain, router, w_gate, w_up, w_down
):
    me = lax.axis_index("expert").astype(jnp.int32).reshape(1)
    gain = norm_gain
    router_t = router[0].T
    weights = (w_gate[0, 0], w_up[0, 0], w_down[0, 0])
    routes = jnp.concatenate([saved_routes, fwd_routes], axis=1)
    backward = functools.partial(expert_call, backward_kernel, me, backward=True)
    forward = functools.partial(expert_call, forward_kernel, me, backward=False)

    r_sib, r_opp, r_far = swap(routes, 1), swap(routes, 2), swap(routes, 3)
    s_opp = swap(saved_in, 2)
    g_opp = swap(grad_in, 2)
    f_opp = swap(fwd_in, 2)
    s_sib, g_sib, f_sib = swap(saved_in, 1), swap(grad_in, 1), swap(fwd_in, 1)

    b_own, b_sib = backward(
        (saved_in, s_sib, grad_in, g_sib), (routes, r_sib), gain, router_t, *weights
    )
    b_back = swap(b_sib, 1)
    s_opp, f_sib, b_own = lax.optimization_barrier((s_opp, f_sib, b_own))
    s_far = swap(s_opp, 1)
    y_own, y_sib = forward((fwd_in, f_sib), (routes, r_sib), gain, router_t, *weights)
    g_opp, b_back, y_own = lax.optimization_barrier((g_opp, b_back, y_own))
    grad_near = shifted(added(grad_in, b_own, b_back), -1, 0)
    fwd_near = shifted(added(fwd_in, y_own, swap(y_sib, 1)), 1, 0)

    g_far = swap(g_opp, 1)
    b_opp, b_far = backward(
        (s_opp, s_far, g_opp, g_far), (r_opp, r_far), gain, router_t, *weights
    )
    grad_far = shifted(added(b_opp, swap(b_far, 1)), -1, 2)
    f_opp, grad_far_ = lax.optimization_barrier((f_opp, b_opp))
    f_far = swap(f_opp, 1)
    y_opp, y_far = forward((f_opp, f_far), (r_opp, r_far), gain, router_t, *weights)
    fwd_far = shifted(added(y_opp, swap(y_far, 1)), 1, 2)
    return (added(fwd_near, fwd_far), added(grad_near, grad_far))


def solution(mesh):
    in_specs = (
        P(("pipe", "expert"), None),
        P(("pipe", "expert"), None),
        P(("pipe", "expert"), None),
        P(("pipe", "expert"), None),
        P(("pipe", "expert"), None),
        P("pipe", None),
        P("pipe", None, None),
        P("pipe", "expert", None, None),
        P("pipe", "expert", None, None),
        P("pipe", "expert", None, None),
    )
    out_specs = (P(("pipe", "expert"), None), P(("pipe", "expert"), None))
    return jax.shard_map(local, mesh=mesh, in_specs=in_specs, out_specs=out_specs, check_vma=False)
```

```python
import functools

import jax
import jax.numpy as jnp
from jax import lax
from jax.experimental import pallas as pl
from jax.experimental.pallas import tpu as pltpu
from jax.sharding import PartitionSpec as P

EPSILON = 1e-06
LANES = 128
BLOCK = 256
OUT = 896
CHUNK = 64
AHEAD = 6
HALVES = (4, 4)
MOST = (7, 1)
PACK_LIMIT = 56 * 1024 * 1024
VMEM_LIMIT = 30 * 1024 * 1024
NT = (((1,), (1,)), ((), ()))
F32 = jnp.float32
BF16 = jnp.bfloat16


def matmul(a, b):
    return jnp.dot(a, b, preferred_element_type=F32)


def matmul_nt(a, b):
    return lax.dot_general(a, b, NT, preferred_element_type=F32)


def load(src, dst, sem):
    copy = pltpu.make_async_copy(src, dst, sem)
    copy.start()
    return copy


def load_pair(a, b, dst, sems, first):
    rows = a.shape[0]
    return [
        load(a, dst.at[pl.ds(0, rows)], sems.at[first]),
        load(b, dst.at[pl.ds(rows, rows)], sems.at[first + 1]),
    ]


def wait(copies):
    for copy in copies:
        copy.wait()


def spans(parts):
    ends = [sum(p.shape[0] for p in parts[: i + 1]) for i in range(len(parts))]
    return [slice(end - p.shape[0], end) for end, p in zip(ends, parts)]


def columns(ref, first, count):
    return ref.at[:, pl.ds(first, count)]


def normalize_rows(xs, gain_ref, normed, inv):
    for at in range(0, xs.shape[0], CHUNK):
        rows = slice(at, at + CHUNK)
        wide = xs[rows, :].astype(F32)
        r = lax.rsqrt(jnp.mean(wide * wide, axis=-1, keepdims=True) + EPSILON)
        inv[rows, :] = jnp.broadcast_to(r, (CHUNK, LANES))
        normed[rows, :] = (xs[rows, :].astype(F32) * r * gain_ref[...]).astype(BF16)


def routing(me, ids, router_pad, normed, first):
    scores = jax.nn.sigmoid(matmul_nt(normed[...], router_pad[...]))
    column = lax.broadcasted_iota(jnp.int32, scores.shape, 1)
    named = ids[...].astype(F32)
    place = column.astype(F32)
    chosen = (place == named[:, first : first + 1]) | (place == named[:, first + 1 : first + 2])
    chosen = chosen.astype(F32)
    mine = chosen * (column == me).astype(F32)
    summed = jnp.sum(chosen * scores, axis=-1, keepdims=True)
    prob = jnp.sum(mine * scores, axis=-1, keepdims=True) / summed
    return scores, chosen, mine, summed, prob


def forward_kernel(first, *refs):
    if first:
        (me_ref, xa, xb, sa, sb, gain_in, router_in, wg, wu, wd) = refs[:10]
        (*parts, wgv, wuv, wdv, gain, router_pad) = refs[10:19]
        (xs, ids, normed, inv, hid, router, sem_x, sem_w) = refs[19:]
    else:
        (me_ref, xa, xb, sa, sb, wgv, wuv, wdv, gain, router_pad, *parts) = refs[:14]
        (xs, ids, normed, inv, hid, sem_x) = refs[14:]
    rows, width = xa.shape
    hidden = wgv.shape[1]
    blocks = [pl.ds(at, BLOCK) for at in range(0, hidden, BLOCK)]
    outs = [pl.ds(at, OUT) for at in range(0, width, OUT)]

    def weights(step):
        if not first:
            return []
        if step < len(blocks):
            at = (slice(None), blocks[step])
            return [
                load(wg.at[at], wgv.at[at], sem_w.at[2 * step]),
                load(wu.at[at], wuv.at[at], sem_w.at[2 * step + 1]),
            ]
        at = (slice(None), outs[step - len(blocks)])
        return [load(wd.at[at], wdv.at[at], sem_w.at[len(blocks) + step])]

    steps = len(blocks) + len(outs)
    loads_x = load_pair(xa, xb, xs, sem_x, 0)
    loads_x += load_pair(columns(sa, width, LANES), columns(sb, width, LANES), ids, sem_x, 2)
    if first:
        loads_r = load(router_in, router, sem_x.at[5])
        loads_x.append(load(gain_in, gain, sem_x.at[4]))
        router_pad[...] = jnp.zeros_like(router_pad)
        loads_r.wait()
        router_pad[0 : router.shape[0], :] = router[...]
    loads_w = [weights(step) for step in range(AHEAD)]
    wait(loads_x)
    normalize_rows(xs, gain, normed, inv)
    prob = routing(me_ref[0], ids, router_pad, normed, 2)[4]
    for step in range(steps):
        wait(loads_w[step])
        if step + AHEAD < steps:
            loads_w.append(weights(step + AHEAD))
        if step < len(blocks):
            at = blocks[step]
            gate = matmul(normed[...], wgv[:, at])
            up = matmul(normed[...], wuv[:, at])
            hid[:, at] = (jax.nn.silu(gate) * up).astype(BF16)
        else:
            at = outs[step - len(blocks)]
            out = prob * matmul(hid[...], wdv[:, at]).astype(BF16).astype(F32)
            for o_ref, src in zip(parts, spans(parts)):
                value = out[src]
                if first and src.start < rows:
                    value += xs[src, at].astype(F32)
                o_ref[:, at] = value.astype(o_ref.dtype)


def gates_kernel(
    me_ref, sa, sb, wgv, wuv, gain, router_pad, gates, ups, stats, slopes,
    xs, ids, normed, sem_x,
):
    width, hidden = wgv.shape
    blocks = [pl.ds(at, BLOCK) for at in range(0, hidden, BLOCK)]
    loads_x = load_pair(columns(sa, 0, width), columns(sb, 0, width), xs, sem_x, 0)
    loads_x += load_pair(columns(sa, width, LANES), columns(sb, width, LANES), ids, sem_x, 2)
    wait(loads_x)
    normalize_rows(xs, gain, normed, stats.at[0])
    scores, chosen, mine, summed, prob = routing(me_ref[0], ids, router_pad, normed, 0)
    stats[1] = jnp.broadcast_to(prob, stats.shape[1:])
    routed = jnp.sum(mine, axis=-1, keepdims=True)
    slopes[...] = routed * chosen * (mine - prob) / summed * scores * (1.0 - scores)
    for at in blocks:
        gates[:, at] = matmul(normed[...], wgv[:, at])
        ups[:, at] = matmul(normed[...], wuv[:, at])


def backward_kernel(
    own, sa, sb, za, zb, gates, ups, stats, slopes, wgv, wuv, wdv, gain, router_pad,
    oa, ob, oc, od, xs, zs, dgs, dus, vs, sem_x,
):
    rows, width = za.shape
    hidden = wgv.shape[1]
    blocks = [pl.ds(at, BLOCK) for at in range(0, hidden, BLOCK)]
    outs = [pl.ds(at, OUT) for at in range(0, width, OUT)]
    loads_z = load_pair(za, zb, zs, sem_x, 2)
    loads_x = load_pair(columns(sa, 0, width), columns(sb, 0, width), xs, sem_x, 0)
    r = stats[0, :, 0:1]
    prob = stats[1, :, 0:1]
    product = jnp.zeros((2 * rows, 1), F32)
    wait(loads_z)
    for at in blocks:
        dhidden = matmul_nt(zs[...], wdv[at, :])
        gate, up = gates[:, at], ups[:, at]
        sig = jax.nn.sigmoid(gate)
        silu = gate * sig
        kept = (silu * up).astype(BF16).astype(F32)
        product += jnp.sum(kept * dhidden, axis=-1, keepdims=True)
        dgs[:, at] = (dhidden * up * sig * (1.0 + gate * (1.0 - sig))).astype(BF16)
        dus[:, at] = (dhidden * silu).astype(BF16)
    dlogits = (slopes[...] * product.astype(BF16).astype(F32)).astype(BF16)
    mean = jnp.zeros((2 * rows, 1), F32)
    wait(loads_x)
    for at in outs:
        n = matmul_nt(dgs[...], wgv[at, :]) + matmul_nt(dus[...], wuv[at, :])
        v = (prob * n + matmul(dlogits, router_pad[:, at])) * gain[:, at]
        vs[:, at] = v
        mean += jnp.sum(v * xs[:, at].astype(F32), axis=-1, keepdims=True)
    shrink = r * r * r * (mean / width)
    parts = (oa, ob, oc, od)
    for o_ref, span in zip(parts, spans(parts)):
        for at in range(span.start, span.stop, 16):
            src = slice(at, at + 16)
            value = r[src] * vs[src, :] - xs[src, :].astype(F32) * shrink[src]
            if own and at < rows:
                value += zs[src, :].astype(F32)
            o_ref[at - span.start : at - span.start + 16, :] = value.astype(o_ref.dtype)


def kernel_call(kernel, operands, outs, scratch, limit=VMEM_LIMIT):
    spaces = {
        "any": pl.BlockSpec(memory_space=pl.ANY),
        "vmem": pl.BlockSpec(memory_space=pltpu.VMEM),
        "smem": pl.BlockSpec(memory_space=pltpu.SMEM),
    }
    return pl.pallas_call(
        kernel,
        out_shape=outs,
        in_specs=[spaces[space] for space, _ in operands],
        out_specs=tuple(spaces["vmem"] for _ in outs),
        scratch_shapes=scratch,
        compiler_params=pltpu.CompilerParams(vmem_limit_bytes=limit),
        cost_estimate=pl.CostEstimate(flops=1, bytes_accessed=1, transcendentals=0),
    )(*[operand for _, operand in operands])


def results_of(rows, width, kind, eighths):
    counts = [rows * part // 8 for part in eighths]
    shapes = [jax.ShapeDtypeStruct((count, width), kind) for count in counts]
    return tuple(shapes + [jax.ShapeDtypeStruct((count, width), BF16) for count in counts])


def placed(space, arrays):
    return [(space, array) for array in arrays]


def forward_first(me, pair, saved, gain, router, weights):
    rows, width = pair[0].shape
    hidden, both = weights[0].shape[1], 2 * rows
    copies = 2 * (hidden // BLOCK) + width // OUT
    operands = [("smem", me), *placed("any", (*pair, *saved, gain, router, *weights))]
    outs = results_of(rows, width, F32, HALVES)
    outs += (*weights, gain, jax.ShapeDtypeStruct((LANES, width), BF16))
    outs = tuple(jax.ShapeDtypeStruct(o.shape, o.dtype) for o in outs)
    scratch = [
        pltpu.VMEM((both, width), BF16),
        pltpu.VMEM((both, LANES), BF16),
        pltpu.VMEM((both, width), BF16),
        pltpu.VMEM((both, LANES), F32),
        pltpu.VMEM((both, hidden), BF16),
        pltpu.VMEM(router.shape, BF16),
        pltpu.SemaphoreType.DMA((6,)),
        pltpu.SemaphoreType.DMA((copies,)),
    ]
    results = kernel_call(functools.partial(forward_kernel, True), operands, outs, scratch)
    return results[:4], results[4:]


def forward(me, pair, saved, held):
    rows, width = pair[0].shape
    hidden, both = held[0].shape[1], 2 * rows
    operands = [("smem", me), *placed("any", (*pair, *saved)), *placed("vmem", held)]
    scratch = [
        pltpu.VMEM((both, width), BF16),
        pltpu.VMEM((both, LANES), BF16),
        pltpu.VMEM((both, width), BF16),
        pltpu.VMEM((both, LANES), F32),
        pltpu.VMEM((both, hidden), BF16),
        pltpu.SemaphoreType.DMA((4,)),
    ]
    outs = results_of(rows, width, BF16, HALVES)
    return kernel_call(functools.partial(forward_kernel, False), operands, outs, scratch)


def gates_of(me, saved, held):
    wg, wu, wd, gain, router = held
    width, hidden = wg.shape
    both = 2 * saved[0].shape[0]
    operands = [("smem", me), *placed("any", saved), *placed("vmem", (wg, wu, gain, router))]
    outs = (
        jax.ShapeDtypeStruct((both, hidden), F32),
        jax.ShapeDtypeStruct((both, hidden), F32),
        jax.ShapeDtypeStruct((2, both, LANES), F32),
        jax.ShapeDtypeStruct((both, LANES), F32),
    )
    scratch = [
        pltpu.VMEM((both, width), BF16),
        pltpu.VMEM((both, LANES), BF16),
        pltpu.VMEM((both, width), BF16),
        pltpu.SemaphoreType.DMA((4,)),
    ]
    return kernel_call(gates_kernel, operands, outs, scratch)


def backward(saved, grads, gated, held, own):
    rows, width = grads[0].shape
    hidden, both = held[0].shape[1], 2 * rows
    operands = [*placed("any", (*saved, *grads)), *placed("vmem", (*gated, *held))]
    scratch = [
        pltpu.VMEM((both, width), BF16),
        pltpu.VMEM((both, width), BF16),
        pltpu.VMEM((both, hidden), BF16),
        pltpu.VMEM((both, hidden), BF16),
        pltpu.VMEM((both, width), F32),
        pltpu.SemaphoreType.DMA((4,)),
    ]
    outs = results_of(rows, width, F32 if own else BF16, MOST if own else HALVES)
    return kernel_call(functools.partial(backward_kernel, own), operands, outs, scratch)


def routed_kernel(rows_in, first_in, second_in, out, first, second, sem):
    count, width = rows_in.shape
    copy = load(rows_in, columns(out, 0, width), sem.at[0])
    wait([load(first_in, first, sem.at[1]), load(second_in, second, sem.at[2])])
    top = first.shape[0]
    blank = jnp.zeros((LANES - 2 * top, count), F32)
    table = jnp.concatenate([first[...].astype(F32), second[...].astype(F32), blank], axis=0)
    out[:, width:] = table.T.astype(BF16)
    copy.wait()


def with_routes(rows, first, second):
    count, width = rows.shape
    operands = placed("any", (rows, first.T, second.T))
    out = jax.ShapeDtypeStruct((count, width + LANES), BF16)
    scratch = [
        pltpu.VMEM(first.T.shape, first.dtype),
        pltpu.VMEM(second.T.shape, second.dtype),
        pltpu.SemaphoreType.DMA((3,)),
    ]
    return kernel_call(routed_kernel, operands, (out,), scratch, PACK_LIMIT)[0]


def swap(x, by):
    peers = lax.axis_size("expert")
    return lax.ppermute(x, "expert", [(i, i ^ by) for i in range(peers)])


def shifted(x, by, across):
    groups, peers = lax.axis_size("pipe"), lax.axis_size("expert")
    pairs = [
        (c * peers + i, (c + by) * peers + (i ^ across))
        for c in range(groups)
        if 0 <= c + by < groups
        for i in range(peers)
    ]
    return lax.ppermute(x, ("pipe", "expert"), pairs)


def joined(*parts):
    return jnp.concatenate(parts, axis=0)


def added(*parts):
    total = parts[0].astype(F32)
    for part in parts[1:]:
        total = total + part.astype(F32)
    return total.astype(BF16)


def local(
    fwd_in, fwd_routes, saved_in, saved_routes, grad_in, norm_gain, router, w_gate, w_up, w_down
):
    me = lax.axis_index("expert").astype(jnp.int32).reshape(1)
    weights = (w_gate[0, 0], w_up[0, 0], w_down[0, 0])
    after = lax.optimization_barrier
    saved = with_routes(saved_in, saved_routes, fwd_routes)

    s_opp, g_opp, f_opp = swap(saved, 2), swap(grad_in, 2), swap(fwd_in, 2)
    f_sib, s_sib, g_sib = swap(fwd_in, 1), swap(saved, 1), swap(grad_in, 1)

    y, held = forward_first(
        me, (fwd_in, f_sib), (saved, s_sib), norm_gain, router[0].T, weights
    )
    y_back = swap(y[2], 1), swap(y[3], 1)
    own_gated = gates_of(me, (saved, s_sib), held)
    s_opp, g_sib, y_back, own_gated = after((s_opp, g_sib, y_back, own_gated))
    s_far = swap(s_opp, 1)
    fwd_near = joined(added(y[0], y_back[0]), added(y[1], y_back[1]))
    fwd_near = shifted(fwd_near, 1, 0)
    b = backward((saved, s_sib), (grad_in, g_sib), own_gated, held, True)
    b_back = swap(b[2], 1), swap(b[3], 1)

    s_far, b = after((s_far, b))
    far_gated = gates_of(me, (s_opp, s_far), held)
    g_opp, b_back, fwd_near, far_gated = after((g_opp, b_back, fwd_near, far_gated))
    g_far = swap(g_opp, 1)
    near_top = shifted(added(b[0], b_back[0]), -1, 0)
    near_low = shifted(added(b[1], b_back[1]), -1, 0)
    b = backward((s_opp, s_far), (g_opp, g_far), far_gated, held, False)
    f_opp, near_top, b = after((f_opp, near_top, b))
    f_far = swap(f_opp, 1)
    grad_far = joined(added(b[0], swap(b[2], 1)), added(b[1], swap(b[3], 1)))
    f_far, grad_far = after((f_far, grad_far))
    grad_far = shifted(grad_far, -1, 2)
    y = forward(me, (f_opp, f_far), (s_opp, s_far), held)
    y, grad_far, near_low = after((y, grad_far, near_low))
    fwd_far = joined(added(y[0], swap(y[2], 1)), added(y[1], swap(y[3], 1)))
    fwd_far = shifted(fwd_far, 1, 2)
    return (added(fwd_near, fwd_far), added(joined(near_top, near_low), grad_far))


def solution(mesh):
    in_specs = (
        P(("pipe", "expert"), None),
        P(("pipe", "expert"), None),
        P(("pipe", "expert"), None),
        P(("pipe", "expert"), None),
        P(("pipe", "expert"), None),
        P("pipe", None),
        P("pipe", None, None),
        P("pipe", "expert", None, None),
        P("pipe", "expert", None, None),
        P("pipe", "expert", None, None),
    )
    out_specs = (P(("pipe", "expert"), None), P(("pipe", "expert"), None))
    return jax.shard_map(local, mesh=mesh, in_specs=in_specs, out_specs=out_specs, check_vma=False)
```

```python
import functools

import jax
import jax.numpy as jnp
from jax import lax
from jax.experimental import pallas as pl
from jax.experimental.pallas import tpu as pltpu
from jax.sharding import PartitionSpec as P

EPSILON = 1e-06
LANES = 128
BLOCK = 256
OUT = 896
CHUNK = 64
AHEAD = 6
HALVES = (4, 4)
MOST = (7, 1)
WIDE = 1792
PACK_LIMIT = 56 * 1024 * 1024
VMEM_LIMIT = 30 * 1024 * 1024
NT = (((1,), (1,)), ((), ()))
F32 = jnp.float32
BF16 = jnp.bfloat16


def matmul(a, b):
    return jnp.dot(a, b, preferred_element_type=F32)


def matmul_nt(a, b):
    return lax.dot_general(a, b, NT, preferred_element_type=F32)


def load(src, dst, sem):
    copy = pltpu.make_async_copy(src, dst, sem)
    copy.start()
    return copy


def load_pair(a, b, dst, sems, first):
    rows = a.shape[0]
    return [
        load(a, dst.at[pl.ds(0, rows)], sems.at[first]),
        load(b, dst.at[pl.ds(rows, rows)], sems.at[first + 1]),
    ]


def wait(copies):
    for copy in copies:
        copy.wait()


def spans(parts):
    ends = [sum(p.shape[0] for p in parts[: i + 1]) for i in range(len(parts))]
    return [slice(end - p.shape[0], end) for end, p in zip(ends, parts)]


def columns(ref, first, count):
    return ref.at[:, pl.ds(first, count)]


def normalize_rows(xs, gain_ref, normed, inv):
    for at in range(0, xs.shape[0], CHUNK):
        rows = slice(at, at + CHUNK)
        wide = xs[rows, :].astype(F32)
        r = lax.rsqrt(jnp.mean(wide * wide, axis=-1, keepdims=True) + EPSILON)
        inv[rows, :] = jnp.broadcast_to(r, (CHUNK, LANES))
        normed[rows, :] = (xs[rows, :].astype(F32) * r * gain_ref[...]).astype(BF16)


def routing(me, ids, router_pad, normed, first):
    scores = jax.nn.sigmoid(matmul_nt(normed[...], router_pad[...]))
    column = lax.broadcasted_iota(jnp.int32, scores.shape, 1)
    named = ids[...].astype(F32)
    place = column.astype(F32)
    chosen = (place == named[:, first : first + 1]) | (place == named[:, first + 1 : first + 2])
    chosen = chosen.astype(F32)
    mine = chosen * (column == me).astype(F32)
    summed = jnp.sum(chosen * scores, axis=-1, keepdims=True)
    prob = jnp.sum(mine * scores, axis=-1, keepdims=True) / summed
    return scores, chosen, mine, summed, prob


def forward_kernel(first, *refs):
    if first:
        (me_ref, xa, xb, sa, sb, gain_in, router_in, wg, wu, wd) = refs[:10]
        (*parts, wgv, wuv, wdv, gain, router_pad) = refs[10:19]
        (xs, ids, normed, inv, hid, router, sem_x, sem_w) = refs[19:]
    else:
        (me_ref, xa, xb, sa, sb, wgv, wuv, wdv, gain, router_pad, *parts) = refs[:14]
        (xs, ids, normed, inv, hid, sem_x) = refs[14:]
    rows, width = xa.shape
    hidden = wgv.shape[1]
    blocks = [pl.ds(at, BLOCK) for at in range(0, hidden, BLOCK)]
    outs = [pl.ds(at, OUT) for at in range(0, width, OUT)]

    def weights(step):
        if not first:
            return []
        if step < len(blocks):
            at = (slice(None), blocks[step])
            return [
                load(wg.at[at], wgv.at[at], sem_w.at[2 * step]),
                load(wu.at[at], wuv.at[at], sem_w.at[2 * step + 1]),
            ]
        at = (slice(None), outs[step - len(blocks)])
        return [load(wd.at[at], wdv.at[at], sem_w.at[len(blocks) + step])]

    steps = len(blocks) + len(outs)
    loads_x = load_pair(xa, xb, xs, sem_x, 0)
    loads_x += load_pair(columns(sa, width, LANES), columns(sb, width, LANES), ids, sem_x, 2)
    if first:
        loads_r = load(router_in, router, sem_x.at[5])
        loads_x.append(load(gain_in, gain, sem_x.at[4]))
        router_pad[...] = jnp.zeros_like(router_pad)
        loads_r.wait()
        router_pad[0 : router.shape[0], :] = router[...]
    loads_w = [weights(step) for step in range(AHEAD)]
    wait(loads_x)
    normalize_rows(xs, gain, normed, inv)
    prob = routing(me_ref[0], ids, router_pad, normed, 2)[4]
    for step in range(steps):
        wait(loads_w[step])
        if step + AHEAD < steps:
            loads_w.append(weights(step + AHEAD))
        if step < len(blocks):
            at = blocks[step]
            gate = matmul(normed[...], wgv[:, at])
            up = matmul(normed[...], wuv[:, at])
            hid[:, at] = (jax.nn.silu(gate) * up).astype(BF16)
        else:
            at = outs[step - len(blocks)]
            out = prob * matmul(hid[...], wdv[:, at]).astype(BF16).astype(F32)
            for o_ref, src in zip(parts, spans(parts)):
                value = out[src]
                if first and src.start < rows:
                    value += xs[src, at].astype(F32)
                o_ref[:, at] = value.astype(o_ref.dtype)


def gates_kernel(
    me_ref, sa, sb, wgv, wuv, gain, router_pad, gates, ups, stats, slopes,
    xs, ids, normed, sem_x,
):
    width, hidden = wgv.shape
    blocks = [pl.ds(at, BLOCK) for at in range(0, hidden, BLOCK)]
    loads_x = load_pair(columns(sa, 0, width), columns(sb, 0, width), xs, sem_x, 0)
    loads_x += load_pair(columns(sa, width, LANES), columns(sb, width, LANES), ids, sem_x, 2)
    wait(loads_x)
    normalize_rows(xs, gain, normed, stats.at[0])
    scores, chosen, mine, summed, prob = routing(me_ref[0], ids, router_pad, normed, 0)
    stats[1] = jnp.broadcast_to(prob, stats.shape[1:])
    routed = jnp.sum(mine, axis=-1, keepdims=True)
    slopes[...] = routed * chosen * (mine - prob) / summed * scores * (1.0 - scores)
    for at in blocks:
        gates[:, at] = matmul(normed[...], wgv[:, at])
        ups[:, at] = matmul(normed[...], wuv[:, at])


def backward_kernel(
    own, sa, sb, za, zb, gates, ups, stats, slopes, wgv, wuv, wdv, gain, router_pad,
    oa, ob, oc, od, xs, zs, dgs, dus, vs, sem_x,
):
    rows, width = za.shape
    hidden = wgv.shape[1]
    blocks = [pl.ds(at, BLOCK) for at in range(0, hidden, BLOCK)]
    outs = [pl.ds(at, WIDE) for at in range(0, width, WIDE)]
    loads_z = load_pair(za, zb, zs, sem_x, 2)
    loads_x = load_pair(columns(sa, 0, width), columns(sb, 0, width), xs, sem_x, 0)
    r = stats[0, :, 0:1]
    prob = stats[1, :, 0:1]
    product = jnp.zeros((2 * rows, 1), F32)
    wait(loads_z)
    for at in blocks:
        dhidden = matmul_nt(zs[...], wdv[at, :])
        gate, up = gates[:, at], ups[:, at]
        sig = jax.nn.sigmoid(gate)
        silu = gate * sig
        kept = (silu * up).astype(BF16).astype(F32)
        product += jnp.sum(kept * dhidden, axis=-1, keepdims=True)
        dgs[:, at] = (dhidden * up * sig * (1.0 + gate * (1.0 - sig))).astype(BF16)
        dus[:, at] = (dhidden * silu).astype(BF16)
    dlogits = (slopes[...] * product.astype(BF16).astype(F32)).astype(BF16)
    mean = jnp.zeros((2 * rows, 1), F32)
    wait(loads_x)
    for at in outs:
        n = matmul_nt(dgs[...], wgv[at, :]) + matmul_nt(dus[...], wuv[at, :])
        v = (prob * n + matmul(dlogits, router_pad[:, at])) * gain[:, at]
        vs[:, at] = v
        mean += jnp.sum(v * xs[:, at].astype(F32), axis=-1, keepdims=True)
    shrink = r * r * r * (mean / width)
    parts = (oa, ob, oc, od)
    for o_ref, span in zip(parts, spans(parts)):
        for at in range(span.start, span.stop, 16):
            src = slice(at, at + 16)
            value = r[src] * vs[src, :] - xs[src, :].astype(F32) * shrink[src]
            if own and at < rows:
                value += zs[src, :].astype(F32)
            o_ref[at - span.start : at - span.start + 16, :] = value.astype(o_ref.dtype)


def kernel_call(kernel, operands, outs, scratch, limit=VMEM_LIMIT):
    spaces = {
        "any": pl.BlockSpec(memory_space=pl.ANY),
        "vmem": pl.BlockSpec(memory_space=pltpu.VMEM),
        "smem": pl.BlockSpec(memory_space=pltpu.SMEM),
    }
    return pl.pallas_call(
        kernel,
        out_shape=outs,
        in_specs=[spaces[space] for space, _ in operands],
        out_specs=tuple(spaces["vmem"] for _ in outs),
        scratch_shapes=scratch,
        compiler_params=pltpu.CompilerParams(vmem_limit_bytes=limit),
        cost_estimate=pl.CostEstimate(flops=1, bytes_accessed=1, transcendentals=0),
    )(*[operand for _, operand in operands])


def results_of(rows, width, kind, eighths):
    counts = [rows * part // 8 for part in eighths]
    shapes = [jax.ShapeDtypeStruct((count, width), kind) for count in counts]
    return tuple(shapes + [jax.ShapeDtypeStruct((count, width), BF16) for count in counts])


def placed(space, arrays):
    return [(space, array) for array in arrays]


def forward_first(me, pair, saved, gain, router, weights):
    rows, width = pair[0].shape
    hidden, both = weights[0].shape[1], 2 * rows
    copies = 2 * (hidden // BLOCK) + width // OUT
    operands = [("smem", me), *placed("any", (*pair, *saved, gain, router, *weights))]
    outs = results_of(rows, width, F32, HALVES)
    outs += (*weights, gain, jax.ShapeDtypeStruct((LANES, width), BF16))
    outs = tuple(jax.ShapeDtypeStruct(o.shape, o.dtype) for o in outs)
    scratch = [
        pltpu.VMEM((both, width), BF16),
        pltpu.VMEM((both, LANES), BF16),
        pltpu.VMEM((both, width), BF16),
        pltpu.VMEM((both, LANES), F32),
        pltpu.VMEM((both, hidden), BF16),
        pltpu.VMEM(router.shape, BF16),
        pltpu.SemaphoreType.DMA((6,)),
        pltpu.SemaphoreType.DMA((copies,)),
    ]
    results = kernel_call(functools.partial(forward_kernel, True), operands, outs, scratch)
    return results[:4], results[4:]


def forward(me, pair, saved, held):
    rows, width = pair[0].shape
    hidden, both = held[0].shape[1], 2 * rows
    operands = [("smem", me), *placed("any", (*pair, *saved)), *placed("vmem", held)]
    scratch = [
        pltpu.VMEM((both, width), BF16),
        pltpu.VMEM((both, LANES), BF16),
        pltpu.VMEM((both, width), BF16),
        pltpu.VMEM((both, LANES), F32),
        pltpu.VMEM((both, hidden), BF16),
        pltpu.SemaphoreType.DMA((4,)),
    ]
    outs = results_of(rows, width, BF16, HALVES)
    return kernel_call(functools.partial(forward_kernel, False), operands, outs, scratch)


def gates_of(me, saved, held):
    wg, wu, wd, gain, router = held
    width, hidden = wg.shape
    both = 2 * saved[0].shape[0]
    operands = [("smem", me), *placed("any", saved), *placed("vmem", (wg, wu, gain, router))]
    outs = (
        jax.ShapeDtypeStruct((both, hidden), F32),
        jax.ShapeDtypeStruct((both, hidden), F32),
        jax.ShapeDtypeStruct((2, both, LANES), F32),
        jax.ShapeDtypeStruct((both, LANES), F32),
    )
    scratch = [
        pltpu.VMEM((both, width), BF16),
        pltpu.VMEM((both, LANES), BF16),
        pltpu.VMEM((both, width), BF16),
        pltpu.SemaphoreType.DMA((4,)),
    ]
    return kernel_call(gates_kernel, operands, outs, scratch)


def backward(saved, grads, gated, held, own):
    rows, width = grads[0].shape
    hidden, both = held[0].shape[1], 2 * rows
    operands = [*placed("any", (*saved, *grads)), *placed("vmem", (*gated, *held))]
    scratch = [
        pltpu.VMEM((both, width), BF16),
        pltpu.VMEM((both, width), BF16),
        pltpu.VMEM((both, hidden), BF16),
        pltpu.VMEM((both, hidden), BF16),
        pltpu.VMEM((both, width), F32),
        pltpu.SemaphoreType.DMA((4,)),
    ]
    outs = results_of(rows, width, F32 if own else BF16, MOST if own else HALVES)
    return kernel_call(functools.partial(backward_kernel, own), operands, outs, scratch)


def routed_kernel(rows_in, first_in, second_in, out, first, second, sem):
    count, width = rows_in.shape
    copy = load(rows_in, columns(out, 0, width), sem.at[0])
    wait([load(first_in, first, sem.at[1]), load(second_in, second, sem.at[2])])
    top = first.shape[0]
    blank = jnp.zeros((LANES - 2 * top, count), F32)
    table = jnp.concatenate([first[...].astype(F32), second[...].astype(F32), blank], axis=0)
    out[:, width:] = table.T.astype(BF16)
    copy.wait()


def with_routes(rows, first, second):
    count, width = rows.shape
    operands = placed("any", (rows, first.T, second.T))
    out = jax.ShapeDtypeStruct((count, width + LANES), BF16)
    scratch = [
        pltpu.VMEM(first.T.shape, first.dtype),
        pltpu.VMEM(second.T.shape, second.dtype),
        pltpu.SemaphoreType.DMA((3,)),
    ]
    return kernel_call(routed_kernel, operands, (out,), scratch, PACK_LIMIT)[0]


def swap(x, by):
    peers = lax.axis_size("expert")
    return lax.ppermute(x, "expert", [(i, i ^ by) for i in range(peers)])


def shifted(x, by, across):
    groups, peers = lax.axis_size("pipe"), lax.axis_size("expert")
    pairs = [
        (c * peers + i, (c + by) * peers + (i ^ across))
        for c in range(groups)
        if 0 <= c + by < groups
        for i in range(peers)
    ]
    return lax.ppermute(x, ("pipe", "expert"), pairs)


def joined(*parts):
    return jnp.concatenate(parts, axis=0)


def added(*parts):
    total = parts[0].astype(F32)
    for part in parts[1:]:
        total = total + part.astype(F32)
    return total.astype(BF16)


def local(
    fwd_in, fwd_routes, saved_in, saved_routes, grad_in, norm_gain, router, w_gate, w_up, w_down
):
    me = lax.axis_index("expert").astype(jnp.int32).reshape(1)
    weights = (w_gate[0, 0], w_up[0, 0], w_down[0, 0])
    after = lax.optimization_barrier
    saved = with_routes(saved_in, saved_routes, fwd_routes)

    s_opp, g_opp, f_opp = swap(saved, 2), swap(grad_in, 2), swap(fwd_in, 2)
    f_sib, s_sib, g_sib = swap(fwd_in, 1), swap(saved, 1), swap(grad_in, 1)

    y, held = forward_first(
        me, (fwd_in, f_sib), (saved, s_sib), norm_gain, router[0].T, weights
    )
    y_back = swap(y[2], 1), swap(y[3], 1)
    own_gated = gates_of(me, (saved, s_sib), held)
    s_opp, g_sib, y_back, own_gated = after((s_opp, g_sib, y_back, own_gated))
    s_far = swap(s_opp, 1)
    fwd_near = joined(added(y[0], y_back[0]), added(y[1], y_back[1]))
    fwd_near = shifted(fwd_near, 1, 0)
    b = backward((saved, s_sib), (grad_in, g_sib), own_gated, held, True)
    b_back = swap(b[2], 1), swap(b[3], 1)

    s_far, b = after((s_far, b))
    far_gated = gates_of(me, (s_opp, s_far), held)
    g_opp, b_back, fwd_near, far_gated = after((g_opp, b_back, fwd_near, far_gated))
    g_far = swap(g_opp, 1)
    near_top = shifted(added(b[0], b_back[0]), -1, 0)
    near_low = shifted(added(b[1], b_back[1]), -1, 0)
    b = backward((s_opp, s_far), (g_opp, g_far), far_gated, held, False)
    f_opp, near_top, marker = after((f_opp, near_top, b[0]))
    b = (marker, *b[1:])
    f_far = swap(f_opp, 1)
    grad_far = joined(added(b[0], swap(b[2], 1)), added(b[1], swap(b[3], 1)))
    f_far, grad_far = after((f_far, grad_far))
    grad_far = shifted(grad_far, -1, 2)
    y = forward(me, (f_opp, f_far), (s_opp, s_far), held)
    y, grad_far, near_low = after((y, grad_far, near_low))
    fwd_far = joined(added(y[0], swap(y[2], 1)), added(y[1], swap(y[3], 1)))
    fwd_far = shifted(fwd_far, 1, 2)
    return (added(fwd_near, fwd_far), added(joined(near_top, near_low), grad_far))


def solution(mesh):
    in_specs = (
        P(("pipe", "expert"), None),
        P(("pipe", "expert"), None),
        P(("pipe", "expert"), None),
        P(("pipe", "expert"), None),
        P(("pipe", "expert"), None),
        P("pipe", None),
        P("pipe", None, None),
        P("pipe", "expert", None, None),
        P("pipe", "expert", None, None),
        P("pipe", "expert", None, None),
    )
    out_specs = (P(("pipe", "expert"), None), P(("pipe", "expert"), None))
    return jax.shard_map(local, mesh=mesh, in_specs=in_specs, out_specs=out_specs, check_vma=False)
```

```python
import functools

import jax
import jax.numpy as jnp
from jax import lax
from jax.experimental import pallas as pl
from jax.experimental.pallas import tpu as pltpu
from jax.sharding import PartitionSpec as P

EPSILON = 1e-06
LANES = 128
BLOCK = 256
OUT = 896
CHUNK = 64
AHEAD = 6
HALVES = (4, 4)
MOST = (7, 1)
WIDE = 1792
PACK_LIMIT = 56 * 1024 * 1024
VMEM_LIMIT = 30 * 1024 * 1024
NT = (((1,), (1,)), ((), ()))
F32 = jnp.float32
BF16 = jnp.bfloat16


def matmul(a, b):
    return jnp.dot(a, b, preferred_element_type=F32)


def matmul_nt(a, b):
    return lax.dot_general(a, b, NT, preferred_element_type=F32)


def load(src, dst, sem):
    copy = pltpu.make_async_copy(src, dst, sem)
    copy.start()
    return copy


def load_pair(a, b, dst, sems, first):
    rows = a.shape[0]
    return [
        load(a, dst.at[pl.ds(0, rows)], sems.at[first]),
        load(b, dst.at[pl.ds(rows, rows)], sems.at[first + 1]),
    ]


def wait(copies):
    for copy in copies:
        copy.wait()


def spans(parts):
    ends = [sum(p.shape[0] for p in parts[: i + 1]) for i in range(len(parts))]
    return [slice(end - p.shape[0], end) for end, p in zip(ends, parts)]


def columns(ref, first, count):
    return ref.at[:, pl.ds(first, count)]


def normalize_rows(xs, gain_ref, normed, inv):
    for at in range(0, xs.shape[0], CHUNK):
        rows = slice(at, at + CHUNK)
        wide = xs[rows, :].astype(F32)
        r = lax.rsqrt(jnp.mean(wide * wide, axis=-1, keepdims=True) + EPSILON)
        inv[rows, :] = jnp.broadcast_to(r, (CHUNK, LANES))
        normed[rows, :] = (xs[rows, :].astype(F32) * r * gain_ref[...]).astype(BF16)


def routing(me, ids, router_pad, normed, first):
    scores = jax.nn.sigmoid(matmul_nt(normed[...], router_pad[...]))
    column = lax.broadcasted_iota(jnp.int32, scores.shape, 1)
    named = ids[...].astype(F32)
    place = column.astype(F32)
    chosen = (place == named[:, first : first + 1]) | (place == named[:, first + 1 : first + 2])
    chosen = chosen.astype(F32)
    mine = chosen * (column == me).astype(F32)
    summed = jnp.sum(chosen * scores, axis=-1, keepdims=True)
    prob = jnp.sum(mine * scores, axis=-1, keepdims=True) / summed
    return scores, chosen, mine, summed, prob


def forward_kernel(first, *refs):
    if first:
        (me_ref, xa, xb, sa, sb, gain_in, router_in, wg, wu, wd) = refs[:10]
        (*parts, wgv, wuv, wdv, gain, router_pad) = refs[10:19]
        (xs, ids, normed, inv, hid, router, sem_x, sem_w) = refs[19:]
    else:
        (me_ref, xa, xb, sa, sb, wgv, wuv, wdv, gain, router_pad, *parts) = refs[:14]
        (xs, ids, normed, inv, hid, sem_x) = refs[14:]
    rows, width = xa.shape
    hidden = wgv.shape[1]
    blocks = [pl.ds(at, BLOCK) for at in range(0, hidden, BLOCK)]
    outs = [pl.ds(at, OUT) for at in range(0, width, OUT)]

    def weights(step):
        if not first:
            return []
        if step < len(blocks):
            at = (slice(None), blocks[step])
            return [
                load(wg.at[at], wgv.at[at], sem_w.at[2 * step]),
                load(wu.at[at], wuv.at[at], sem_w.at[2 * step + 1]),
            ]
        at = (slice(None), outs[step - len(blocks)])
        return [load(wd.at[at], wdv.at[at], sem_w.at[len(blocks) + step])]

    steps = len(blocks) + len(outs)
    loads_x = load_pair(xa, xb, xs, sem_x, 0)
    loads_x += load_pair(columns(sa, width, LANES), columns(sb, width, LANES), ids, sem_x, 2)
    if first:
        loads_r = load(router_in, router, sem_x.at[5])
        loads_x.append(load(gain_in, gain, sem_x.at[4]))
        router_pad[...] = jnp.zeros_like(router_pad)
        loads_r.wait()
        router_pad[0 : router.shape[0], :] = router[...]
    loads_w = [weights(step) for step in range(AHEAD)]
    wait(loads_x)
    normalize_rows(xs, gain, normed, inv)
    prob = routing(me_ref[0], ids, router_pad, normed, 2)[4]
    for step in range(steps):
        wait(loads_w[step])
        if step + AHEAD < steps:
            loads_w.append(weights(step + AHEAD))
        if step < len(blocks):
            at = blocks[step]
            gate = matmul(normed[...], wgv[:, at])
            up = matmul(normed[...], wuv[:, at])
            hid[:, at] = (jax.nn.silu(gate) * up).astype(BF16)
        else:
            at = outs[step - len(blocks)]
            out = prob * matmul(hid[...], wdv[:, at]).astype(BF16).astype(F32)
            for o_ref, src in zip(parts, spans(parts)):
                value = out[src]
                if first and src.start < rows:
                    value += xs[src, at].astype(F32)
                o_ref[:, at] = value.astype(o_ref.dtype)


def gates_kernel(
    me_ref, sa, sb, wgv, wuv, gain, router_pad, gates, ups, stats, slopes,
    xs, ids, normed, sem_x,
):
    width, hidden = wgv.shape
    blocks = [pl.ds(at, BLOCK) for at in range(0, hidden, BLOCK)]
    loads_x = load_pair(columns(sa, 0, width), columns(sb, 0, width), xs, sem_x, 0)
    loads_x += load_pair(columns(sa, width, LANES), columns(sb, width, LANES), ids, sem_x, 2)
    wait(loads_x)
    normalize_rows(xs, gain, normed, stats.at[0])
    scores, chosen, mine, summed, prob = routing(me_ref[0], ids, router_pad, normed, 0)
    stats[1] = jnp.broadcast_to(prob, stats.shape[1:])
    routed = jnp.sum(mine, axis=-1, keepdims=True)
    slopes[...] = routed * chosen * (mine - prob) / summed * scores * (1.0 - scores)
    for at in blocks:
        gates[:, at] = matmul(normed[...], wgv[:, at])
        ups[:, at] = matmul(normed[...], wuv[:, at])


def backward_kernel(
    own, sa, sb, za, zb, gates, ups, stats, slopes, wgv, wuv, wdv, gain, router_pad,
    oa, ob, oc, od, xs, zs, dgs, dus, vs, sem_x,
):
    rows, width = za.shape
    hidden = wgv.shape[1]
    blocks = [pl.ds(at, BLOCK) for at in range(0, hidden, BLOCK)]
    outs = [pl.ds(at, WIDE) for at in range(0, width, WIDE)]
    loads_z = load_pair(za, zb, zs, sem_x, 2)
    loads_x = load_pair(columns(sa, 0, width), columns(sb, 0, width), xs, sem_x, 0)
    r = stats[0, :, 0:1]
    prob = stats[1, :, 0:1]
    product = jnp.zeros((2 * rows, 1), F32)
    wait(loads_z)
    for at in blocks:
        dhidden = matmul_nt(zs[...], wdv[at, :])
        gate, up = gates[:, at], ups[:, at]
        sig = jax.nn.sigmoid(gate)
        silu = gate * sig
        kept = (silu * up).astype(BF16).astype(F32)
        product += jnp.sum(kept * dhidden, axis=-1, keepdims=True)
        dgs[:, at] = (dhidden * up * sig * (1.0 + gate * (1.0 - sig))).astype(BF16)
        dus[:, at] = (dhidden * silu).astype(BF16)
    dlogits = (slopes[...] * product.astype(BF16).astype(F32)).astype(BF16)
    mean = jnp.zeros((2 * rows, 1), F32)
    wait(loads_x)
    for at in outs:
        n = matmul_nt(dgs[...], wgv[at, :]) + matmul_nt(dus[...], wuv[at, :])
        v = (prob * n + matmul(dlogits, router_pad[:, at])) * gain[:, at]
        vs[:, at] = v
        mean += jnp.sum(v * xs[:, at].astype(F32), axis=-1, keepdims=True)
    shrink = r * r * r * (mean / width)
    parts = (oa, ob, oc, od)
    for o_ref, span in zip(parts, spans(parts)):
        for at in range(span.start, span.stop, 16):
            src = slice(at, at + 16)
            value = r[src] * vs[src, :] - xs[src, :].astype(F32) * shrink[src]
            if own and at < rows:
                value += zs[src, :].astype(F32)
            o_ref[at - span.start : at - span.start + 16, :] = value.astype(o_ref.dtype)


def kernel_call(kernel, operands, outs, scratch, limit=VMEM_LIMIT):
    spaces = {
        "any": pl.BlockSpec(memory_space=pl.ANY),
        "vmem": pl.BlockSpec(memory_space=pltpu.VMEM),
        "smem": pl.BlockSpec(memory_space=pltpu.SMEM),
    }
    return pl.pallas_call(
        kernel,
        out_shape=outs,
        in_specs=[spaces[space] for space, _ in operands],
        out_specs=tuple(spaces["vmem"] for _ in outs),
        scratch_shapes=scratch,
        compiler_params=pltpu.CompilerParams(vmem_limit_bytes=limit),
        cost_estimate=pl.CostEstimate(flops=1, bytes_accessed=1, transcendentals=0),
    )(*[operand for _, operand in operands])


def results_of(rows, width, kind, eighths):
    counts = [rows * part // 8 for part in eighths]
    shapes = [jax.ShapeDtypeStruct((count, width), kind) for count in counts]
    return tuple(shapes + [jax.ShapeDtypeStruct((count, width), BF16) for count in counts])


def placed(space, arrays):
    return [(space, array) for array in arrays]


def forward_first(me, pair, saved, gain, router, weights):
    rows, width = pair[0].shape
    hidden, both = weights[0].shape[1], 2 * rows
    copies = 2 * (hidden // BLOCK) + width // OUT
    operands = [("smem", me), *placed("any", (*pair, *saved, gain, router, *weights))]
    outs = results_of(rows, width, F32, HALVES)
    outs += (*weights, gain, jax.ShapeDtypeStruct((LANES, width), BF16))
    outs = tuple(jax.ShapeDtypeStruct(o.shape, o.dtype) for o in outs)
    scratch = [
        pltpu.VMEM((both, width), BF16),
        pltpu.VMEM((both, LANES), BF16),
        pltpu.VMEM((both, width), BF16),
        pltpu.VMEM((both, LANES), F32),
        pltpu.VMEM((both, hidden), BF16),
        pltpu.VMEM(router.shape, BF16),
        pltpu.SemaphoreType.DMA((6,)),
        pltpu.SemaphoreType.DMA((copies,)),
    ]
    results = kernel_call(functools.partial(forward_kernel, True), operands, outs, scratch)
    return results[:4], results[4:]


def forward(me, pair, saved, held):
    rows, width = pair[0].shape
    hidden, both = held[0].shape[1], 2 * rows
    operands = [("smem", me), *placed("any", (*pair, *saved)), *placed("vmem", held)]
    scratch = [
        pltpu.VMEM((both, width), BF16),
        pltpu.VMEM((both, LANES), BF16),
        pltpu.VMEM((both, width), BF16),
        pltpu.VMEM((both, LANES), F32),
        pltpu.VMEM((both, hidden), BF16),
        pltpu.SemaphoreType.DMA((4,)),
    ]
    outs = results_of(rows, width, BF16, HALVES)
    return kernel_call(functools.partial(forward_kernel, False), operands, outs, scratch)


def gates_of(me, saved, held):
    wg, wu, wd, gain, router = held
    width, hidden = wg.shape
    both = 2 * saved[0].shape[0]
    operands = [("smem", me), *placed("any", saved), *placed("vmem", (wg, wu, gain, router))]
    outs = (
        jax.ShapeDtypeStruct((both, hidden), F32),
        jax.ShapeDtypeStruct((both, hidden), F32),
        jax.ShapeDtypeStruct((2, both, LANES), F32),
        jax.ShapeDtypeStruct((both, LANES), F32),
    )
    scratch = [
        pltpu.VMEM((both, width), BF16),
        pltpu.VMEM((both, LANES), BF16),
        pltpu.VMEM((both, width), BF16),
        pltpu.SemaphoreType.DMA((4,)),
    ]
    return kernel_call(gates_kernel, operands, outs, scratch)


def backward(saved, grads, gated, held, own):
    rows, width = grads[0].shape
    hidden, both = held[0].shape[1], 2 * rows
    operands = [*placed("any", (*saved, *grads)), *placed("vmem", (*gated, *held))]
    scratch = [
        pltpu.VMEM((both, width), BF16),
        pltpu.VMEM((both, width), BF16),
        pltpu.VMEM((both, hidden), BF16),
        pltpu.VMEM((both, hidden), BF16),
        pltpu.VMEM((both, width), F32),
        pltpu.SemaphoreType.DMA((4,)),
    ]
    outs = results_of(rows, width, F32 if own else BF16, MOST if own else HALVES)
    return kernel_call(functools.partial(backward_kernel, own), operands, outs, scratch)


def routed_kernel(rows_in, first_in, second_in, out, first, second, sem):
    count, width = rows_in.shape
    copy = load(rows_in, columns(out, 0, width), sem.at[0])
    wait([load(first_in, first, sem.at[1]), load(second_in, second, sem.at[2])])
    top = first.shape[0]
    blank = jnp.zeros((LANES - 2 * top, count), F32)
    table = jnp.concatenate([first[...].astype(F32), second[...].astype(F32), blank], axis=0)
    out[:, width:] = table.T.astype(BF16)
    copy.wait()


def with_routes(rows, first, second):
    count, width = rows.shape
    operands = placed("any", (rows, first.T, second.T))
    out = jax.ShapeDtypeStruct((count, width + LANES), BF16)
    scratch = [
        pltpu.VMEM(first.T.shape, first.dtype),
        pltpu.VMEM(second.T.shape, second.dtype),
        pltpu.SemaphoreType.DMA((3,)),
    ]
    return kernel_call(routed_kernel, operands, (out,), scratch, PACK_LIMIT)[0]


def swap(x, by):
    peers = lax.axis_size("expert")
    return lax.ppermute(x, "expert", [(i, i ^ by) for i in range(peers)])


def shifted(x, by, across):
    groups, peers = lax.axis_size("pipe"), lax.axis_size("expert")
    pairs = [
        (c * peers + i, (c + by) * peers + (i ^ across))
        for c in range(groups)
        if 0 <= c + by < groups
        for i in range(peers)
    ]
    return lax.ppermute(x, ("pipe", "expert"), pairs)


def joined(*parts):
    return jnp.concatenate(parts, axis=0)


def added(*parts):
    total = parts[0].astype(F32)
    for part in parts[1:]:
        total = total + part.astype(F32)
    return total.astype(BF16)


def local(
    fwd_in, fwd_routes, saved_in, saved_routes, grad_in, norm_gain, router, w_gate, w_up, w_down
):
    me = lax.axis_index("expert").astype(jnp.int32).reshape(1)
    weights = (w_gate[0, 0], w_up[0, 0], w_down[0, 0])
    after = lax.optimization_barrier
    saved = with_routes(saved_in, saved_routes, fwd_routes)

    s_opp, g_opp, f_opp = swap(saved, 2), swap(grad_in, 2), swap(fwd_in, 2)
    f_sib, s_sib, g_sib = swap(fwd_in, 1), swap(saved, 1), swap(grad_in, 1)

    y, held = forward_first(
        me, (fwd_in, f_sib), (saved, s_sib), norm_gain, router[0].T, weights
    )
    y_back = swap(y[2], 1), swap(y[3], 1)
    own_gated = gates_of(me, (saved, s_sib), held)
    s_opp, g_sib, y_back, own_gated = after((s_opp, g_sib, y_back, own_gated))
    s_far = swap(s_opp, 1)
    fwd_near = joined(added(y[0], y_back[0]), added(y[1], y_back[1]))
    fwd_near = shifted(fwd_near, 1, 0)
    b = backward((saved, s_sib), (grad_in, g_sib), own_gated, held, True)
    b_back = swap(b[2], 1), swap(b[3], 1)

    s_far, b = after((s_far, b))
    far_gated = gates_of(me, (s_opp, s_far), held)
    g_opp, b_back, fwd_near, far_gated = after((g_opp, b_back, fwd_near, far_gated))
    g_far = swap(g_opp, 1)
    near_top = shifted(added(b[0], b_back[0]), -1, 0)
    near_low = shifted(added(b[1], b_back[1]), -1, 0)
    b = backward((s_opp, s_far), (g_opp, g_far), far_gated, held, False)
    f_opp, near_top, marker = after((f_opp, near_top, b[0]))
    b = (marker, *b[1:])
    f_far = swap(f_opp, 1)
    grad_far = joined(added(b[0], swap(b[2], 1)), added(b[1], swap(b[3], 1)))
    s_far, grad_far = after((s_far, grad_far))
    grad_far = shifted(grad_far, -1, 2)
    y = forward(me, (f_opp, f_far), (s_opp, s_far), held)
    y, grad_far, near_low = after((y, grad_far, near_low))
    fwd_far = joined(added(y[0], swap(y[2], 1)), added(y[1], swap(y[3], 1)))
    fwd_far = shifted(fwd_far, 1, 2)
    return (added(fwd_near, fwd_far), added(joined(near_top, near_low), grad_far))


def solution(mesh):
    in_specs = (
        P(("pipe", "expert"), None),
        P(("pipe", "expert"), None),
        P(("pipe", "expert"), None),
        P(("pipe", "expert"), None),
        P(("pipe", "expert"), None),
        P("pipe", None),
        P("pipe", None, None),
        P("pipe", "expert", None, None),
        P("pipe", "expert", None, None),
        P("pipe", "expert", None, None),
    )
    out_specs = (P(("pipe", "expert"), None), P(("pipe", "expert"), None))
    return jax.shard_map(local, mesh=mesh, in_specs=in_specs, out_specs=out_specs, check_vma=False)
```
